32 devices in a mesh: dp: 8 (over z, core), seq: 4 (over y, x).
Axes of the slice: x: 2, y: 2, z: 4, core: 2. Of those that a mesh axis runs over, the one named last changes fastest.
Arguments:
- tokens: bfloat16 [8, 1024, 1024], P('dp', 'seq'), may hold values from -6 to 6
- out_grad: bfloat16 [8, 1024, 1024], P('dp', 'seq'), may hold values from -6 to 6
- alibi_slopes: float32 [16], replicated, as said below
- qkv_weight: bfloat16 [1024, 3072], P(('dp', 'seq')), may hold values from -0.1875 to 0.1875
- dense_weight: bfloat16 [1024, 1024], P(('dp', 'seq')), may hold values from -0.75 to 0.75
- fc1_weight: bfloat16 [1024, 4096], P(('dp', 'seq')), may hold values from -0.1875 to 0.1875
- fc2_weight: bfloat16 [4096, 1024], P(('dp', 'seq')), may hold values from -0.09375 to 0.09375
- norm_gains: bfloat16 [2, 1024], P(None, ('dp', 'seq')), may hold values from 0.5 to 1.5
- biases: bfloat16 [6, 1024], P(None, ('dp', 'seq')), may hold values from -3 to 3
- fc1_bias: bfloat16 [4096], P(('dp', 'seq')), may hold values from -3 to 3
Outputs:
- layer_out: bfloat16 [8, 1024, 1024], P('dp', 'seq')
- tokens_grad: bfloat16 [8, 1024, 1024], P('dp', 'seq')
- qkv_grad: float32 [1024, 3072], P(('dp', 'seq'))
- dense_grad: float32 [1024, 1024], P(('dp', 'seq'))
- fc1_grad: float32 [1024, 4096], P(('dp', 'seq'))
- fc2_grad: float32 [4096, 1024], P(('dp', 'seq'))
- gains_grad: float32 [2, 1024], P(None, ('dp', 'seq'))
- biases_grad: float32 [6, 1024], P(None, ('dp', 'seq'))
- fc1_bias_grad: float32 [4096], P(('dp', 'seq'))
The draws below stay inside these ranges and needn't reach their ends.
Inputs may be any that keep to these rules, and one draw needn't show every extreme that they name: `alibi_slopes`: each head's slope is positive, between 0.2 / 1024 and 0.1.
All inputs are finite; a program needn't handle non-finite values.
Results may differ from the reference program's by a relative error of at most 0.013.
Values may be sent and summed in bfloat16 or wider, within the bound.
A program may use at most 192 MiB of HBM per device.

```python
import math
import jax
import jax.numpy as jnp
from jax import lax

HEADS = 16
HEAD_DIM = 64
FF = 4096
D = 1024
LENGTH = 1024
SEQS = 8


def draw_alibi_slopes(key, part):
    key = jax.random.fold_in(key, 11)
    picked = jax.random.uniform(key, (HEADS,), jnp.float32)
    lower_end = math.log(0.5 / LENGTH)
    upper_end = math.log(0.1)
    return jnp.exp(lower_end + (upper_end - lower_end) * picked)


def shard_levels(stream_key, extent, pieces, least, largest):
    factor_of, own = 1.0, jax.random.fold_in(stream_key, 6)
    for position, blocks in pieces:
        heights = jnp.exp(jax.random.uniform(jax.random.fold_in(own, position), (blocks,), jnp.float32, least / len(pieces), largest / len(pieces)))
        factor_of = factor_of * jnp.repeat(heights, extent[position] // blocks).reshape([-1 if axis == position else 1 for axis in range(len(extent))])
    return factor_of


def scatter_about(rng, shape, deviation, most, split=(), kind=jnp.bfloat16):
    gain = shard_levels(rng, shape, split, -0.22, 0.18) if split else 1.0
    entries = jax.random.normal(rng, shape, jnp.float32) * deviation * gain
    return jnp.minimum(jnp.maximum(entries, -most), most).astype(kind)


def setup_inputs(seed: int = 0) -> dict:
    keys = jax.random.split(jax.random.key(seed), 11)
    return {
        "tokens": scatter_about(keys[0], (SEQS, LENGTH, D), 1.0, 6.0, ((0, 8), (1, 4))),
        "out_grad": scatter_about(keys[1], (SEQS, LENGTH, D), 1.0, 6.0, ((0, 8), (1, 4))),
        "alibi_slopes": draw_alibi_slopes(jax.random.fold_in(keys[10], 71), 0),
        "qkv_weight": scatter_about(keys[3], (D, 3 * D), D ** -0.5, 0.1875, ((0, 32),)),
        "dense_weight": scatter_about(keys[4], (D, D), (D // 16) ** -0.5, 0.75, ((0, 32),)),
        "fc1_weight": scatter_about(keys[5], (D, FF), D ** -0.5, 0.1875, ((0, 32),)),
        "fc2_weight": scatter_about(keys[6], (FF, D), FF ** -0.5, 0.09375, ((0, 32),)),
        "norm_gains": jnp.clip(1.0 + 0.1 * jax.random.normal(keys[7], (2, D), jnp.float32), 0.5, 1.5).astype(jnp.bfloat16),
        "biases": scatter_about(keys[8], (6, D), 0.5, 3.0, ((1, 32),)),
        "fc1_bias": scatter_about(keys[9], (FF,), 0.5, 3.0, ((0, 32),)),
    }


best_precision = lax.Precision.HIGHEST

@jax.custom_vjp
def low(v):
    return lax.optimization_barrier(v.astype(jnp.bfloat16)).astype(jnp.float32)

@jax.custom_vjp
def low_back(v):
    return v

def low_keep(v):
    return (low(v), None)

def low_pass(kept, grad):
    return (grad,)

def back_keep(v):
    return (v, None)

def back_low(kept, grad):
    return (low(grad),)
low.defvjp(low_keep, low_pass)
low_back.defvjp(back_keep, back_low)

def layer_norm(values, gain_vec, shift_vec):
    row_mean = lax.optimization_barrier(jnp.mean(values, axis=-1, keepdims=True))
    centred = values - row_mean
    spread = lax.optimization_barrier(jnp.mean(centred * centred, axis=-1, keepdims=True))
    return centred * lax.rsqrt(spread + 1e-05) * gain_vec + shift_vec

def attend_rows(query_blk, row_start, key_rows, value_rows, slopes):
    scores = jnp.einsum('qhe,khe->hqk', query_blk, key_rows, precision=best_precision) * HEAD_DIM ** (-0.5)
    q_pos = row_start + jnp.arange(query_blk.shape[0], dtype=jnp.int32)
    k_pos = jnp.arange(key_rows.shape[0], dtype=jnp.int32)
    distance = (q_pos[:, None] - k_pos[None, :]).astype(jnp.float32)
    scores = scores - slopes[:, None, None] * distance[None]
    scores = low_back(jnp.where(distance[None] >= 0, scores, -1e+30))
    prob_vals = jnp.exp(scores - jax.nn.logsumexp(scores, axis=-1, keepdims=True))
    return jnp.einsum('hqk,khe->qhe', low(prob_vals), value_rows, precision=best_precision)

def layer_forward(sequence, slopes, w_qkv, w_dense, w_fc1, w_fc2, gains, shifts, fc1_shift):
    model_width = HEADS * HEAD_DIM
    h_one = low(layer_norm(sequence, gains[0], shifts[0]))
    proj_bias = jnp.concatenate([shifts[1], jnp.zeros_like(shifts[1]), shifts[2]])
    projected = low(low_back(jnp.dot(h_one, w_qkv, precision=best_precision) + proj_bias))
    heads_all = projected.reshape(LENGTH, 3, HEADS, HEAD_DIM)
    query_rows = heads_all[:, 0]
    key_rows = heads_all[:, 1]
    value_rows = heads_all[:, 2]
    blk_rows = min(512, LENGTH)
    count_blk = LENGTH // blk_rows
    query_blks = query_rows.reshape(count_blk, blk_rows, HEADS, HEAD_DIM)
    row_starts = jnp.arange(count_blk, dtype=jnp.int32) * blk_rows
    attend = jax.checkpoint(attend_rows)
    attended = lax.map(lambda pair_in: attend(pair_in[0], pair_in[1], key_rows, value_rows, slopes), (query_blks, row_starts))
    attended = low(low_back(attended.reshape(LENGTH, model_width)))
    residual = sequence + low_back(jnp.dot(attended, w_dense, precision=best_precision) + shifts[3])
    h_two = low(layer_norm(residual, gains[1], shifts[4]))
    upper = low_back(jnp.dot(h_two, w_fc1, precision=best_precision) + fc1_shift)
    activated = low(jax.nn.gelu(upper, approximate=True))
    return residual + jnp.dot(activated, w_fc2, precision=best_precision) + shifts[5]

def reference(tokens, out_grad, alibi_slopes, qkv_weight, dense_weight, fc1_weight, fc2_weight, norm_gains, biases, fc1_bias):
    params = tuple((weight_arr.astype(jnp.float32) for weight_arr in (qkv_weight, dense_weight, fc1_weight, fc2_weight, norm_gains, biases, fc1_bias)))
    slopes = alibi_slopes.astype(jnp.float32)

    def per_sequence(carry, pair_in):
        sequence, cotangent = pair_in
        result, pull_back = jax.vjp(lambda seq_in, *weights: layer_forward(seq_in, slopes, *weights), sequence.astype(jnp.float32), *params)
        grads = pull_back(cotangent.astype(jnp.float32))
        carry = tuple((running + part_grad for running, part_grad in zip(carry, grads[1:])))
        return (carry, (result.astype(jnp.bfloat16), grads[0].astype(jnp.bfloat16)))
    start_sums = tuple((jnp.zeros(weight_arr.shape, jnp.float32) for weight_arr in params))
    sums, (layer_out, tokens_grad) = lax.scan(per_sequence, start_sums, (tokens, out_grad))
    return (layer_out, tokens_grad, sums[0], sums[1], sums[2], sums[3], sums[4], sums[5], sums[6])
```

```python
import jax
import jax.numpy as jnp
from jax import lax
from jax.sharding import PartitionSpec as P

HEADS = 16
HEAD_DIM = 64


epsilon = 1e-05
negative = -1e30
low = jnp.bfloat16
wide = jnp.float32


def layer_norm(values, gain_vec, shift_vec):
    row_mean = jnp.mean(values, axis=-1, keepdims=True)
    centred = values - row_mean
    spread = jnp.mean(centred * centred, axis=-1, keepdims=True)
    return centred * lax.rsqrt(spread + epsilon) * gain_vec + shift_vec


def gelu_tanh(values):
    return jax.nn.gelu(values, approximate=True)


def dot(spec, left, right):
    return jnp.einsum(spec, left, right, preferred_element_type=wide)


def gather_seq(rows):
    return lax.all_gather(rows, "seq", axis=0, tiled=True)


def scatter_seq(rows):
    return lax.psum_scatter(rows, "seq", scatter_dimension=0, tiled=True).astype(wide)


def swap_seq(chunks):
    return lax.all_to_all(chunks, "seq", split_axis=0, concat_axis=0, tiled=True)


def gather_dp(rows):
    return lax.all_gather(rows, "dp", axis=0, tiled=True)


def scatter_dp(rows):
    return lax.psum_scatter(rows, "dp", scatter_dimension=0, tiled=True)


def attention_forward(q_heads, k_heads, v_heads, slopes, block):
    length = q_heads.shape[1]
    kept, outs = [], []
    for start in range(0, length, block):
        end = start + block
        scores = dot("hqe,hke->hqk", q_heads[:, start:end], k_heads[:, :end]) * HEAD_DIM ** (-0.5)
        q_pos = start + lax.broadcasted_iota(jnp.int32, (block, end), 0)
        k_pos = lax.broadcasted_iota(jnp.int32, (block, end), 1)
        distance = (q_pos - k_pos).astype(wide)
        scores = scores - slopes[:, None, None] * distance[None]
        scores = jnp.where(distance[None] >= 0, scores, negative)
        weights = jnp.exp(scores - jnp.max(scores, axis=-1, keepdims=True))
        total = jnp.sum(weights, axis=-1, keepdims=True)
        probs = (weights * (1.0 / total)).astype(low)
        kept.append(probs)
        outs.append(dot("hqk,hke->hqe", probs, v_heads[:, :end]))
    return jnp.concatenate(outs, axis=1), kept


def attention_backward(q_heads, k_heads, v_heads, g_heads, delta, kept, block):
    length = q_heads.shape[1]
    grad_q = []
    grad_k = jnp.zeros(k_heads.shape, wide)
    grad_v = jnp.zeros(v_heads.shape, wide)
    for index, start in enumerate(range(0, length, block)):
        end = start + block
        probs = kept[index]
        g_blk = g_heads[:, start:end]
        q_blk = q_heads[:, start:end]
        grad_probs = dot("hqe,hke->hqk", g_blk, v_heads[:, :end])
        grad_scores = (
            probs.astype(wide) * (grad_probs - delta[:, start:end, None]) * HEAD_DIM ** (-0.5)
        ).astype(low)
        grad_q.append(dot("hqk,hke->hqe", grad_scores, k_heads[:, :end]))
        grad_k = grad_k.at[:, :end].add(dot("hqk,hqe->hke", grad_scores, q_blk))
        grad_v = grad_v.at[:, :end].add(dot("hqk,hqe->hke", probs, g_blk))
    return jnp.concatenate(grad_q, axis=1), grad_k, grad_v


def body(
    tokens,
    out_grad,
    alibi_slopes,
    qkv_weight,
    dense_weight,
    fc1_weight,
    fc2_weight,
    norm_gains,
    biases,
    fc1_bias,
):
    n_dp, n_seq = lax.axis_size("dp"), lax.axis_size("seq")
    parts = n_dp * n_seq
    my_dp, my_seq = lax.axis_index("dp"), lax.axis_index("seq")
    me = my_dp * n_seq + my_seq
    width = HEADS * HEAD_DIM
    rows, length = tokens.shape[1], tokens.shape[1] * n_seq
    local_heads = HEADS // n_seq
    cols = width // n_seq
    w_rows = qkv_weight.shape[0]
    ff_rows = fc2_weight.shape[0]
    units = ff_rows * n_dp
    block = min(256, length)
    spread = [(b, (b % n_dp) * n_seq + b // n_dp) for b in range(parts)]
    back = [(there, b) for b, there in spread]

    small = jnp.concatenate([norm_gains.reshape(-1), biases.reshape(-1), fc1_bias])
    small = lax.all_gather(small, ("dp", "seq"), axis=0, tiled=False)
    vec = small[:, : 8 * w_rows].reshape(parts, 8, w_rows).transpose(1, 0, 2).reshape(8, width)
    vec = vec.astype(wide)
    gains, shifts = vec[:2], vec[2:]
    ff_bias = small[:, 8 * w_rows :].reshape(n_dp, n_seq, ff_rows)
    ff_bias = lax.dynamic_index_in_dim(ff_bias, my_seq, 1, keepdims=False).reshape(units)
    ff_bias = ff_bias.astype(wide)

    part_qkv = qkv_weight.reshape(w_rows, 3, n_seq, cols).transpose(2, 0, 1, 3)
    part_qkv = swap_seq(part_qkv.reshape(n_seq, w_rows, 3 * cols))
    w_qkv = gather_dp(part_qkv.reshape(n_seq * w_rows, 3 * cols))
    w_dense = gather_dp(lax.ppermute(dense_weight, ("dp", "seq"), spread))
    part_fc1 = fc1_weight.reshape(w_rows, n_dp, n_seq, ff_rows).transpose(2, 0, 1, 3)
    part_fc1 = swap_seq(part_fc1.reshape(n_seq, w_rows, units))
    w_fc1 = gather_dp(part_fc1.reshape(n_seq * w_rows, units))
    w_fc2 = gather_dp(fc2_weight)

    inputs = tokens[0].astype(wide)
    normed_one, norm_pull_one = jax.vjp(layer_norm, inputs, gains[0], shifts[0])
    h_one = gather_seq(normed_one.astype(low))
    dy = out_grad[0]
    dy_all = gather_seq(dy)

    def my_cols(row):
        return lax.dynamic_slice_in_dim(row, my_seq * cols, cols, 0)

    proj_bias = jnp.concatenate([my_cols(shifts[1]), jnp.zeros((cols,), wide), my_cols(shifts[2])])
    projected = (dot("td,dc->tc", h_one, w_qkv) + proj_bias).astype(low)
    heads_first = projected.reshape(length, 3, local_heads, HEAD_DIM).transpose(1, 2, 0, 3)
    q_heads, k_heads, v_heads = heads_first[0], heads_first[1], heads_first[2]
    slopes = lax.dynamic_slice_in_dim(alibi_slopes, my_seq * local_heads, local_heads, 0)
    attended, kept = attention_forward(q_heads, k_heads, v_heads, slopes, block)
    attended_low = attended.astype(low).transpose(1, 0, 2).reshape(length, cols)
    branch = scatter_seq(dot("tc,cd->td", attended_low, w_dense).astype(low))
    residual = inputs + branch + shifts[3]
    normed_two, norm_pull_two = jax.vjp(layer_norm, residual, gains[1], shifts[4])
    h_two = gather_seq(normed_two.astype(low))
    upper = dot("td,df->tf", h_two, w_fc1) + ff_bias
    activated, gelu_pull = jax.vjp(gelu_tanh, upper)
    act_low = activated.astype(low)
    grad_act = dot("td,fd->tf", dy_all, w_fc2)
    grad_upper = gelu_pull(grad_act)[0].astype(low)
    grad_h_two = scatter_seq(dot("tf,df->td", grad_upper, w_fc1).astype(low))
    layer_out = (
        residual + scatter_seq(dot("tf,fd->td", act_low, w_fc2).astype(low)) + shifts[5]
    ).astype(low)
    grad_fc2 = scatter_dp(dot("tf,td->fd", act_low, dy_all).astype(low))
    grad_fc1 = scatter_dp(dot("td,tf->df", h_two, grad_upper).astype(low))
    grad_fc1_bias = jnp.sum(grad_upper, axis=0, dtype=wide)

    grad_res_norm, grad_gain_two, grad_shift_two = norm_pull_two(grad_h_two)
    grad_resid = dy.astype(wide) + grad_res_norm
    grad_branch = grad_resid.astype(low)
    branch_all = gather_seq(grad_branch)
    grad_dense = scatter_dp(dot("tc,td->cd", attended_low, branch_all).astype(low))
    grad_attended = dot("td,cd->tc", branch_all, w_dense).astype(low)
    g_heads = grad_attended.reshape(length, local_heads, HEAD_DIM).transpose(1, 0, 2)
    delta = jnp.sum(g_heads.astype(wide) * attended, axis=-1)
    grad_q, grad_k, grad_v = attention_backward(
        q_heads, k_heads, v_heads, g_heads, delta, kept, block
    )
    grad_proj = jnp.stack([grad_q, grad_k, grad_v]).astype(low)
    grad_proj = grad_proj.transpose(2, 0, 1, 3).reshape(length, 3 * cols)
    grad_h_one = scatter_seq(dot("tc,dc->td", grad_proj, w_qkv).astype(low))
    grad_qkv = scatter_dp(dot("td,tc->dc", h_one, grad_proj).astype(low))
    proj_sums = jnp.sum(grad_proj, axis=0, dtype=wide)

    def place(values):
        return lax.dynamic_update_slice_in_dim(jnp.zeros((width,), wide), values, my_seq * cols, 0)

    grad_in_norm, grad_gain_one, grad_shift_one = norm_pull_one(grad_h_one)
    tokens_grad = (grad_resid + grad_in_norm).astype(low)[None]
    ff_placed = lax.dynamic_update_slice_in_dim(
        jnp.zeros((n_dp, n_seq, ff_rows), wide),
        grad_fc1_bias.reshape(n_dp, 1, ff_rows),
        my_seq,
        1,
    )
    vec_sums = jnp.stack(
        [
            grad_gain_one,
            grad_gain_two,
            grad_shift_one,
            place(proj_sums[:cols]),
            place(proj_sums[2 * cols :]),
            jnp.sum(grad_branch, axis=0, dtype=wide),
            grad_shift_two,
            jnp.sum(dy, axis=0, dtype=wide),
        ]
    )
    sums = lax.psum(jnp.concatenate([vec_sums.reshape(-1), ff_placed.reshape(-1)]), ("dp", "seq"))
    vec_sums = lax.dynamic_slice_in_dim(sums[: 8 * width].reshape(8, width), me * w_rows, w_rows, 1)
    fc1_bias_grad = lax.dynamic_slice_in_dim(sums, 8 * width + me * ff_rows, ff_rows, 0)

    out_fc1 = swap_seq(grad_fc1.reshape(n_seq, w_rows, units))
    out_fc1 = out_fc1.reshape(n_seq, w_rows, n_dp, ff_rows).transpose(1, 2, 0, 3)
    out_qkv = swap_seq(grad_qkv.reshape(n_seq, w_rows, 3 * cols))
    out_qkv = out_qkv.reshape(n_seq, w_rows, 3, cols).transpose(1, 2, 0, 3)
    out_dense = lax.ppermute(grad_dense, ("dp", "seq"), back)
    return (
        layer_out[None],
        tokens_grad,
        out_qkv.reshape(w_rows, 3 * width).astype(wide),
        out_dense.astype(wide),
        out_fc1.reshape(w_rows, units * n_seq).astype(wide),
        grad_fc2.astype(wide),
        vec_sums[:2],
        vec_sums[2:],
        fc1_bias_grad,
    )


def solution(mesh):
    return jax.shard_map(
        body,
        mesh=mesh,
        in_specs=(
            P("dp", "seq", None),
            P("dp", "seq", None),
            P(),
            P(("dp", "seq"), None),
            P(("dp", "seq"), None),
            P(("dp", "seq"), None),
            P(("dp", "seq"), None),
            P(None, ("dp", "seq")),
            P(None, ("dp", "seq")),
            P(("dp", "seq")),
        ),
        out_specs=(
            P("dp", "seq", None),
            P("dp", "seq", None),
            P(("dp", "seq"), None),
            P(("dp", "seq"), None),
            P(("dp", "seq"), None),
            P(("dp", "seq"), None),
            P(None, ("dp", "seq")),
            P(None, ("dp", "seq")),
            P(("dp", "seq")),
        ),
        check_vma=False,
    )
```

```python
import functools
import jax
import jax.numpy as jnp
from jax import lax
from jax.experimental import pallas as pl
from jax.experimental.pallas import tpu as pltpu
from jax.sharding import PartitionSpec as P

HEADS = 16
HEAD_DIM = 64


epsilon = 1e-05
negative = -1e30
low = jnp.bfloat16
wide = jnp.float32


def layer_norm(values, gain_vec, shift_vec):
    row_mean = jnp.mean(values, axis=-1, keepdims=True)
    centred = values - row_mean
    spread = jnp.mean(centred * centred, axis=-1, keepdims=True)
    return centred * lax.rsqrt(spread + epsilon) * gain_vec + shift_vec


def gelu_tanh(values):
    return jax.nn.gelu(values, approximate=True)


def dot(spec, left, right):
    return jnp.einsum(spec, left, right, preferred_element_type=wide)


def start_all(copies):
    for copy in copies:
        copy.start()


def greet(targets):
    barrier = pltpu.get_barrier_semaphore()
    for target in targets:
        pl.semaphore_signal(barrier, inc=1, device_id=target, device_id_type=pl.DeviceIdType.MESH)
    pl.semaphore_wait(barrier, len(targets))


def send(src, dst, send_sem, recv_sem, target):
    return pltpu.make_async_remote_copy(
        src_ref=src,
        dst_ref=dst,
        send_sem=send_sem,
        recv_sem=recv_sem,
        device_id=target,
        device_id_type=pl.DeviceIdType.MESH,
    )


def exchange_kernel(count, is_gather, src, out, send_sem, recv_sem, local_sem):
    mine, my_dp = lax.axis_index("seq"), lax.axis_index("dp")
    peers = [lax.rem(mine + step, count) for step in range(1, count)]
    greet([(my_dp, peer) for peer in peers])
    copies = [
        send(
            src if is_gather else src.at[peer],
            out.at[mine],
            send_sem.at[step],
            recv_sem.at[step],
            (my_dp, peer),
        )
        for step, peer in enumerate(peers)
    ]
    start_all(copies)
    local = pltpu.make_async_copy(src if is_gather else src.at[mine], out.at[mine], local_sem)
    local.start()
    local.wait()
    for copy in copies:
        copy.wait()


def exchange(values, number, is_gather):
    count = lax.axis_size("seq")
    shape = (count, *values.shape) if is_gather else values.shape
    return pl.pallas_call(
        functools.partial(exchange_kernel, count, is_gather),
        out_shape=jax.ShapeDtypeStruct(shape, values.dtype),
        in_specs=[pl.BlockSpec(memory_space=pl.ANY)],
        out_specs=pl.BlockSpec(memory_space=pl.ANY),
        scratch_shapes=[
            pltpu.SemaphoreType.DMA((count - 1,)),
            pltpu.SemaphoreType.DMA((count - 1,)),
            pltpu.SemaphoreType.DMA,
        ],
        compiler_params=pltpu.CompilerParams(collective_id=number, has_side_effects=True),
        cost_estimate=pl.CostEstimate(flops=0, bytes_accessed=60_000_000, transcendentals=0),
        name=f"exchange_{number}",
    )(values)


def open_kernel(
    n_z, n_seq, x, dy, up, down, x_all, dy_all, up_all, down_all,
    swap_s, swap_r, x_s, x_r, dy_s, dy_r, up_s, up_r, down_s, down_r, up_ts, up_tr, down_ts, down_tr,
    local_sem,
):
    my_dp, my_seq = lax.axis_index("dp"), lax.axis_index("seq")
    my_z, core = my_dp // 2, lax.rem(my_dp, 2)
    seq_peers = [lax.rem(my_seq + step, n_seq) for step in range(1, n_seq)]
    z_peers = [(lax.rem(my_z + step, n_z) * 2 + core, my_seq) for step in range(1, n_z)]
    twin = (my_z * 2 + 1 - core, my_seq)
    greet([(my_dp, peer) for peer in seq_peers] + z_peers + [twin])
    swaps = [
        send(up.at[p], up_all.at[my_dp, my_seq], swap_s.at[k], swap_r.at[k], (my_dp, p))
        for k, p in enumerate(seq_peers)
    ]
    start_all(swaps)
    downs = [
        send(down, down_all.at[my_dp], down_s.at[k], down_r.at[k], target)
        for k, target in enumerate(z_peers)
    ]
    start_all(downs)
    down_twins = [send(down, down_all.at[my_dp], down_ts.at[0], down_tr.at[0], twin)]
    start_all(down_twins)
    rows = []
    for k, p in enumerate(seq_peers):
        rows.append(send(x, x_all.at[my_seq], x_s.at[k], x_r.at[k], (my_dp, p)))
        rows.append(send(dy, dy_all.at[my_seq], dy_s.at[k], dy_r.at[k], (my_dp, p)))
    start_all(rows)
    own = [
        pltpu.make_async_copy(up.at[my_seq], up_all.at[my_dp, my_seq], local_sem.at[0]),
        pltpu.make_async_copy(down, down_all.at[my_dp], local_sem.at[1]),
        pltpu.make_async_copy(x, x_all.at[my_seq], local_sem.at[2]),
        pltpu.make_async_copy(dy, dy_all.at[my_seq], local_sem.at[3]),
    ]
    start_all(own)
    for copy in own:
        copy.wait()
    for copy in swaps:
        copy.wait()
    ups = [
        send(up_all.at[my_dp], up_all.at[my_dp], up_s.at[k], up_r.at[k], target)
        for k, target in enumerate(z_peers)
    ]
    start_all(ups)
    up_twins = [send(up_all.at[my_dp], up_all.at[my_dp], up_ts.at[0], up_tr.at[0], twin)]
    start_all(up_twins)
    for copies, onward, whole, send_sem, recv_sem in (
        (downs, down_twins, down_all, down_ts, down_tr),
        (ups, up_twins, up_all, up_ts, up_tr),
    ):
        for k in range(1, n_z):
            copies[k - 1].wait_recv()
            slot = lax.rem(my_z + n_z - k, n_z) * 2 + core
            onward.append(send(whole.at[slot], whole.at[slot], send_sem.at[k], recv_sem.at[k], twin))
            onward[-1].start()
    for copy in downs + ups:
        copy.wait_send()
    for copy in down_twins + up_twins + rows:
        copy.wait()


def open_gather(x, dy, up, down):
    n_seq, n_dp = lax.axis_size("seq"), lax.axis_size("dp")
    n_z = n_dp // 2
    sems = [n_seq - 1] * 6 + [n_z - 1] * 4 + [n_z] * 4 + [4]
    return pl.pallas_call(
        functools.partial(open_kernel, n_z, n_seq),
        out_shape=(
            jax.ShapeDtypeStruct((n_seq, *x.shape), x.dtype),
            jax.ShapeDtypeStruct((n_seq, *dy.shape), dy.dtype),
            jax.ShapeDtypeStruct((n_dp, *up.shape), up.dtype),
            jax.ShapeDtypeStruct((n_dp, *down.shape), down.dtype),
        ),
        in_specs=[pl.BlockSpec(memory_space=pl.ANY)] * 4,
        out_specs=[pl.BlockSpec(memory_space=pl.ANY)] * 4,
        scratch_shapes=[pltpu.SemaphoreType.DMA((extent,)) for extent in sems],
        compiler_params=pltpu.CompilerParams(collective_id=0, has_side_effects=True),
        cost_estimate=pl.CostEstimate(flops=0, bytes_accessed=200_000_000, transcendentals=0),
        name="open_gather",
    )(x, dy, up, down)


def total_kernel(n_dp, n_seq, values, out, by_seq, part, by_dp, s_send, s_recv, d_send, d_recv):
    my_dp, my_seq = lax.axis_index("dp"), lax.axis_index("seq")
    seq_peers = [(my_dp, lax.rem(my_seq + step, n_seq)) for step in range(1, n_seq)]
    dp_peers = [(lax.rem(my_dp + step, n_dp), my_seq) for step in range(1, n_dp)]
    greet(seq_peers + dp_peers)
    copies = [
        send(values, by_seq.at[k], s_send.at[k], s_recv.at[k], target)
        for k, target in enumerate(seq_peers)
    ]
    start_all(copies)
    for copy in copies:
        copy.wait()
    part[...] = values[...] + jnp.sum(by_seq[...], axis=0)
    copies = [
        send(part, by_dp.at[k], d_send.at[k], d_recv.at[k], target)
        for k, target in enumerate(dp_peers)
    ]
    start_all(copies)
    for copy in copies:
        copy.wait()
    out[...] = part[...] + jnp.sum(by_dp[...], axis=0)


def total(values, number):
    n_seq, n_dp = lax.axis_size("seq"), lax.axis_size("dp")
    return pl.pallas_call(
        functools.partial(total_kernel, n_dp, n_seq),
        out_shape=jax.ShapeDtypeStruct(values.shape, values.dtype),
        in_specs=[pl.BlockSpec(memory_space=pltpu.VMEM)],
        out_specs=pl.BlockSpec(memory_space=pltpu.VMEM),
        scratch_shapes=[
            pltpu.VMEM((n_seq - 1, *values.shape), values.dtype),
            pltpu.VMEM(values.shape, values.dtype),
            pltpu.VMEM((n_dp - 1, *values.shape), values.dtype),
            pltpu.SemaphoreType.DMA((n_seq - 1,)),
            pltpu.SemaphoreType.DMA((n_seq - 1,)),
            pltpu.SemaphoreType.DMA((n_dp - 1,)),
            pltpu.SemaphoreType.DMA((n_dp - 1,)),
        ],
        compiler_params=pltpu.CompilerParams(collective_id=number, has_side_effects=True),
        cost_estimate=pl.CostEstimate(flops=0, bytes_accessed=40_000_000, transcendentals=0),
        name=f"total_{number}",
    )(values)


def gather_seq(rows, number):
    return exchange(rows, number, True).reshape(-1, rows.shape[-1])


def scatter_seq(rows, number):
    count = lax.axis_size("seq")
    chunks = exchange(rows.reshape(count, -1, rows.shape[-1]), number, False)
    return jnp.sum(chunks.astype(wide), axis=0)


def late_scatter_seq(rows):
    return lax.psum_scatter(rows, "seq", scatter_dimension=0, tiled=True).astype(wide)


def swap_seq(chunks):
    return lax.all_to_all(chunks, "seq", split_axis=0, concat_axis=0, tiled=True)


def gather_dp(rows):
    return lax.all_gather(rows, "dp", axis=0, tiled=True)


def scatter_dp(rows):
    return lax.psum_scatter(rows, "dp", scatter_dimension=0, tiled=True)


def attention_forward(q_heads, k_heads, v_heads, slopes, block):
    length = q_heads.shape[1]
    kept, outs = [], []
    for start in range(0, length, block):
        end = start + block
        scores = dot("hqe,hke->hqk", q_heads[:, start:end], k_heads[:, :end]) * HEAD_DIM ** (-0.5)
        q_pos = start + lax.broadcasted_iota(jnp.int32, (block, end), 0)
        k_pos = lax.broadcasted_iota(jnp.int32, (block, end), 1)
        distance = (q_pos - k_pos).astype(wide)
        scores = scores - slopes[:, None, None] * distance[None]
        scores = jnp.where(distance[None] >= 0, scores, negative)
        weights = jnp.exp(scores - jnp.max(scores, axis=-1, keepdims=True))
        total = jnp.sum(weights, axis=-1, keepdims=True)
        probs = (weights * (1.0 / total)).astype(low)
        kept.append(probs)
        outs.append(dot("hqk,hke->hqe", probs, v_heads[:, :end]))
    return jnp.concatenate(outs, axis=1), kept


def attention_backward(q_heads, k_heads, v_heads, g_heads, delta, kept, block):
    length = q_heads.shape[1]
    grad_q = []
    grad_k = jnp.zeros(k_heads.shape, wide)
    grad_v = jnp.zeros(v_heads.shape, wide)
    for index, start in enumerate(range(0, length, block)):
        end = start + block
        probs = kept[index]
        g_blk = g_heads[:, start:end]
        q_blk = q_heads[:, start:end]
        grad_probs = dot("hqe,hke->hqk", g_blk, v_heads[:, :end])
        grad_scores = (
            probs.astype(wide) * (grad_probs - delta[:, start:end, None]) * HEAD_DIM ** (-0.5)
        ).astype(low)
        grad_q.append(dot("hqk,hke->hqe", grad_scores, k_heads[:, :end]))
        grad_k = grad_k.at[:, :end].add(dot("hqk,hqe->hke", grad_scores, q_blk))
        grad_v = grad_v.at[:, :end].add(dot("hqk,hqe->hke", probs, g_blk))
    return jnp.concatenate(grad_q, axis=1), grad_k, grad_v


def body(
    tokens,
    out_grad,
    alibi_slopes,
    qkv_weight,
    dense_weight,
    fc1_weight,
    fc2_weight,
    norm_gains,
    biases,
    fc1_bias,
):
    n_dp, n_seq = lax.axis_size("dp"), lax.axis_size("seq")
    parts = n_dp * n_seq
    my_dp, my_seq = lax.axis_index("dp"), lax.axis_index("seq")
    me = my_dp * n_seq + my_seq
    width = HEADS * HEAD_DIM
    rows, length = tokens.shape[1], tokens.shape[1] * n_seq
    local_heads = HEADS // n_seq
    cols = width // n_seq
    w_rows = qkv_weight.shape[0]
    ff_rows = fc2_weight.shape[0]
    units = ff_rows * n_dp
    block = min(256, length)
    spread = [(b, (b % n_dp) * n_seq + b // n_dp) for b in range(parts)]
    back = [(there, b) for b, there in spread]

    small = jnp.concatenate([norm_gains.reshape(-1), biases.reshape(-1), fc1_bias])
    small = lax.all_gather(small, ("dp", "seq"), axis=0, tiled=False)
    vec = small[:, : 8 * w_rows].reshape(parts, 8, w_rows).transpose(1, 0, 2).reshape(8, width)
    vec = vec.astype(wide)
    gains, shifts = vec[:2], vec[2:]
    ff_bias = small[:, 8 * w_rows :].reshape(n_dp, n_seq, ff_rows)
    ff_bias = lax.dynamic_index_in_dim(ff_bias, my_seq, 1, keepdims=False).reshape(units)
    ff_bias = ff_bias.astype(wide)

    part_qkv = qkv_weight.reshape(w_rows, 3, n_seq, cols).transpose(2, 0, 1, 3)
    part_fc1 = fc1_weight.reshape(w_rows, n_dp, n_seq, ff_rows).transpose(2, 0, 1, 3)
    up = jnp.concatenate(
        [part_qkv.reshape(n_seq, w_rows, 3 * cols), part_fc1.reshape(n_seq, w_rows, units)], axis=2
    )
    w_dense = gather_dp(lax.ppermute(dense_weight, ("dp", "seq"), spread))
    dy = out_grad[0]
    x_all, dy_all, up_all, w_fc2 = open_gather(tokens[0], dy, up, fc2_weight)
    up_all = up_all.reshape(width, 3 * cols + units)
    w_qkv, w_fc1 = up_all[:, : 3 * cols], up_all[:, 3 * cols :]
    w_fc2 = w_fc2.reshape(units, width)
    dy_all = dy_all.reshape(length, width)

    inputs = tokens[0].astype(wide)
    _, norm_pull_one = jax.vjp(layer_norm, inputs, gains[0], shifts[0])
    x_all = x_all.reshape(length, width).astype(wide)
    h_one = layer_norm(x_all, gains[0], shifts[0]).astype(low)

    def my_cols(row):
        return lax.dynamic_slice_in_dim(row, my_seq * cols, cols, 0)

    proj_bias = jnp.concatenate([my_cols(shifts[1]), jnp.zeros((cols,), wide), my_cols(shifts[2])])
    projected = (dot("td,dc->tc", h_one, w_qkv) + proj_bias).astype(low)
    heads_first = projected.reshape(length, 3, local_heads, HEAD_DIM).transpose(1, 2, 0, 3)
    q_heads, k_heads, v_heads = heads_first[0], heads_first[1], heads_first[2]
    slopes = lax.dynamic_slice_in_dim(alibi_slopes, my_seq * local_heads, local_heads, 0)
    attended, kept = attention_forward(q_heads, k_heads, v_heads, slopes, block)
    attended_low = attended.astype(low).transpose(1, 0, 2).reshape(length, cols)
    branch = scatter_seq(dot("tc,cd->td", attended_low, w_dense).astype(low), 1)
    residual = inputs + branch + shifts[3]
    normed_two, norm_pull_two = jax.vjp(layer_norm, residual, gains[1], shifts[4])
    h_two = gather_seq(normed_two.astype(low), 2)
    upper = dot("td,df->tf", h_two, w_fc1) + ff_bias
    activated, gelu_pull = jax.vjp(gelu_tanh, upper)
    act_low = activated.astype(low)
    grad_act = dot("td,fd->tf", dy_all, w_fc2)
    grad_upper = gelu_pull(grad_act)[0].astype(low)
    grad_h_two = scatter_seq(dot("tf,df->td", grad_upper, w_fc1).astype(low), 3)
    layer_out = (
        residual + late_scatter_seq(dot("tf,fd->td", act_low, w_fc2).astype(low)) + shifts[5]
    ).astype(low)
    grad_fc2 = scatter_dp(dot("tf,td->fd", act_low, dy_all).astype(low))
    grad_fc1 = scatter_dp(dot("td,tf->df", h_two, grad_upper).astype(low))
    grad_fc1_bias = jnp.sum(grad_upper, axis=0, dtype=wide)

    grad_res_norm, grad_gain_two, grad_shift_two = norm_pull_two(grad_h_two)
    grad_resid = dy.astype(wide) + grad_res_norm
    grad_branch = grad_resid.astype(low)
    branch_all = gather_seq(grad_branch, 4)
    grad_dense = scatter_dp(dot("tc,td->cd", attended_low, branch_all).astype(low))
    grad_attended = dot("td,cd->tc", branch_all, w_dense).astype(low)
    g_heads = grad_attended.reshape(length, local_heads, HEAD_DIM).transpose(1, 0, 2)
    delta = jnp.sum(g_heads.astype(wide) * attended, axis=-1)
    grad_q, grad_k, grad_v = attention_backward(
        q_heads, k_heads, v_heads, g_heads, delta, kept, block
    )
    grad_proj = jnp.stack([grad_q, grad_k, grad_v]).astype(low)
    grad_proj = grad_proj.transpose(2, 0, 1, 3).reshape(length, 3 * cols)
    grad_h_one = scatter_seq(dot("tc,dc->td", grad_proj, w_qkv).astype(low), 5)
    grad_qkv = scatter_dp(dot("td,tc->dc", h_one, grad_proj).astype(low))
    proj_sums = jnp.sum(grad_proj, axis=0, dtype=wide)

    def place(values):
        return lax.dynamic_update_slice_in_dim(jnp.zeros((width,), wide), values, my_seq * cols, 0)

    grad_in_norm, grad_gain_one, grad_shift_one = norm_pull_one(grad_h_one)
    tokens_grad = (grad_resid + grad_in_norm).astype(low)[None]
    ff_placed = lax.dynamic_update_slice_in_dim(
        jnp.zeros((n_dp, n_seq, ff_rows), wide),
        grad_fc1_bias.reshape(n_dp, 1, ff_rows),
        my_seq,
        1,
    )
    vec_sums = jnp.stack(
        [
            grad_gain_one,
            grad_gain_two,
            grad_shift_one,
            place(proj_sums[:cols]),
            place(proj_sums[2 * cols :]),
            jnp.sum(grad_branch, axis=0, dtype=wide),
            grad_shift_two,
            jnp.sum(dy, axis=0, dtype=wide),
        ]
    )
    sums = jnp.concatenate([vec_sums.reshape(-1, 128), ff_placed.reshape(-1, 128)])
    sums = total(sums, 6).reshape(-1)
    vec_sums = lax.dynamic_slice_in_dim(sums[: 8 * width].reshape(8, width), me * w_rows, w_rows, 1)
    fc1_bias_grad = lax.dynamic_slice_in_dim(sums, 8 * width + me * ff_rows, ff_rows, 0)

    out_fc1 = swap_seq(grad_fc1.reshape(n_seq, w_rows, units))
    out_fc1 = out_fc1.reshape(n_seq, w_rows, n_dp, ff_rows).transpose(1, 2, 0, 3)
    out_qkv = swap_seq(grad_qkv.reshape(n_seq, w_rows, 3 * cols))
    out_qkv = out_qkv.reshape(n_seq, w_rows, 3, cols).transpose(1, 2, 0, 3)
    out_dense = lax.ppermute(grad_dense, ("dp", "seq"), back)
    return (
        layer_out[None],
        tokens_grad,
        out_qkv.reshape(w_rows, 3 * width).astype(wide),
        out_dense.astype(wide),
        out_fc1.reshape(w_rows, units * n_seq).astype(wide),
        grad_fc2.astype(wide),
        vec_sums[:2],
        vec_sums[2:],
        fc1_bias_grad,
    )


def solution(mesh):
    return jax.shard_map(
        body,
        mesh=mesh,
        in_specs=(
            P("dp", "seq", None),
            P("dp", "seq", None),
            P(),
            P(("dp", "seq"), None),
            P(("dp", "seq"), None),
            P(("dp", "seq"), None),
            P(("dp", "seq"), None),
            P(None, ("dp", "seq")),
            P(None, ("dp", "seq")),
            P(("dp", "seq")),
        ),
        out_specs=(
            P("dp", "seq", None),
            P("dp", "seq", None),
            P(("dp", "seq"), None),
            P(("dp", "seq"), None),
            P(("dp", "seq"), None),
            P(("dp", "seq"), None),
            P(None, ("dp", "seq")),
            P(None, ("dp", "seq")),
            P(("dp", "seq")),
        ),
        check_vma=False,
    )
```

```python
import functools
import jax
import jax.numpy as jnp
from jax import lax
from jax.experimental import pallas as pl
from jax.experimental.pallas import tpu as pltpu
from jax.sharding import PartitionSpec as P

HEADS = 16
HEAD_DIM = 64


epsilon = 1e-05
negative = -1e30
low = jnp.bfloat16
wide = jnp.float32


def layer_norm(values, gain_vec, shift_vec):
    row_mean = jnp.mean(values, axis=-1, keepdims=True)
    centred = values - row_mean
    spread = jnp.mean(centred * centred, axis=-1, keepdims=True)
    return centred * lax.rsqrt(spread + epsilon) * gain_vec + shift_vec


def gelu_tanh(values):
    return jax.nn.gelu(values, approximate=True)


def dot(spec, left, right):
    return jnp.einsum(spec, left, right, preferred_element_type=wide)


def start_all(copies):
    for copy in copies:
        copy.start()


def greet(targets):
    barrier = pltpu.get_barrier_semaphore()
    for target in targets:
        pl.semaphore_signal(barrier, inc=1, device_id=target, device_id_type=pl.DeviceIdType.MESH)
    pl.semaphore_wait(barrier, len(targets))


def send(src, dst, send_sem, recv_sem, target):
    return pltpu.make_async_remote_copy(
        src_ref=src,
        dst_ref=dst,
        send_sem=send_sem,
        recv_sem=recv_sem,
        device_id=target,
        device_id_type=pl.DeviceIdType.MESH,
    )


def exchange_kernel(count, is_gather, src, out, send_sem, recv_sem, local_sem):
    mine, my_dp = lax.axis_index("seq"), lax.axis_index("dp")
    peers = [lax.rem(mine + step, count) for step in range(1, count)]
    greet([(my_dp, peer) for peer in peers])
    copies = [
        send(
            src if is_gather else src.at[peer],
            out.at[mine],
            send_sem.at[step],
            recv_sem.at[step],
            (my_dp, peer),
        )
        for step, peer in enumerate(peers)
    ]
    start_all(copies)
    local = pltpu.make_async_copy(src if is_gather else src.at[mine], out.at[mine], local_sem)
    local.start()
    local.wait()
    for copy in copies:
        copy.wait()


def exchange(values, number, is_gather):
    count = lax.axis_size("seq")
    shape = (count, *values.shape) if is_gather else values.shape
    return pl.pallas_call(
        functools.partial(exchange_kernel, count, is_gather),
        out_shape=jax.ShapeDtypeStruct(shape, values.dtype),
        in_specs=[pl.BlockSpec(memory_space=pl.ANY)],
        out_specs=pl.BlockSpec(memory_space=pl.ANY),
        scratch_shapes=[
            pltpu.SemaphoreType.DMA((count - 1,)),
            pltpu.SemaphoreType.DMA((count - 1,)),
            pltpu.SemaphoreType.DMA,
        ],
        compiler_params=pltpu.CompilerParams(collective_id=number, has_side_effects=True),
        cost_estimate=pl.CostEstimate(flops=0, bytes_accessed=60_000_000, transcendentals=0),
        name=f"exchange_{number}",
    )(values)


def open_kernel(
    n_z, n_seq, x, dy, up, down, x_all, dy_all, up_all, down_all,
    swap_s, swap_r, x_s, x_r, dy_s, dy_r, up_s, up_r, down_s, down_r, up_ts, up_tr, down_ts, down_tr,
    local_sem,
):
    my_dp, my_seq = lax.axis_index("dp"), lax.axis_index("seq")
    my_z, core = my_dp // 2, lax.rem(my_dp, 2)
    seq_peers = [lax.rem(my_seq + step, n_seq) for step in range(1, n_seq)]
    z_peers = [(lax.rem(my_z + step, n_z) * 2 + core, my_seq) for step in range(1, n_z)]
    twin = (my_z * 2 + 1 - core, my_seq)
    greet([(my_dp, peer) for peer in seq_peers] + z_peers + [twin])
    swaps = [
        send(up.at[p], up_all.at[my_dp, my_seq], swap_s.at[k], swap_r.at[k], (my_dp, p))
        for k, p in enumerate(seq_peers)
    ]
    start_all(swaps)
    downs = [
        send(down, down_all.at[my_dp], down_s.at[k], down_r.at[k], target)
        for k, target in enumerate(z_peers)
    ]
    start_all(downs)
    down_twins = [send(down, down_all.at[my_dp], down_ts.at[0], down_tr.at[0], twin)]
    start_all(down_twins)
    rows = []
    for k, p in enumerate(seq_peers):
        rows.append(send(x, x_all.at[my_seq], x_s.at[k], x_r.at[k], (my_dp, p)))
        rows.append(send(dy, dy_all.at[my_seq], dy_s.at[k], dy_r.at[k], (my_dp, p)))
    start_all(rows)
    own = [
        pltpu.make_async_copy(up.at[my_seq], up_all.at[my_dp, my_seq], local_sem.at[0]),
        pltpu.make_async_copy(down, down_all.at[my_dp], local_sem.at[1]),
        pltpu.make_async_copy(x, x_all.at[my_seq], local_sem.at[2]),
        pltpu.make_async_copy(dy, dy_all.at[my_seq], local_sem.at[3]),
    ]
    start_all(own)
    for copy in own:
        copy.wait()
    for copy in swaps:
        copy.wait()
    ups = [
        send(up_all.at[my_dp], up_all.at[my_dp], up_s.at[k], up_r.at[k], target)
        for k, target in enumerate(z_peers)
    ]
    start_all(ups)
    up_twins = [send(up_all.at[my_dp], up_all.at[my_dp], up_ts.at[0], up_tr.at[0], twin)]
    start_all(up_twins)
    for copies, onward, whole, send_sem, recv_sem in (
        (downs, down_twins, down_all, down_ts, down_tr),
        (ups, up_twins, up_all, up_ts, up_tr),
    ):
        for k in range(1, n_z):
            copies[k - 1].wait_recv()
            slot = lax.rem(my_z + n_z - k, n_z) * 2 + core
            onward.append(send(whole.at[slot], whole.at[slot], send_sem.at[k], recv_sem.at[k], twin))
            onward[-1].start()
    for copy in downs + ups:
        copy.wait_send()
    for copy in down_twins + up_twins + rows:
        copy.wait()


def open_gather(x, dy, up, down):
    n_seq, n_dp = lax.axis_size("seq"), lax.axis_size("dp")
    n_z = n_dp // 2
    sems = [n_seq - 1] * 6 + [n_z - 1] * 4 + [n_z] * 4 + [4]
    return pl.pallas_call(
        functools.partial(open_kernel, n_z, n_seq),
        out_shape=(
            jax.ShapeDtypeStruct((n_seq, *x.shape), x.dtype),
            jax.ShapeDtypeStruct((n_seq, *dy.shape), dy.dtype),
            jax.ShapeDtypeStruct((n_dp, *up.shape), up.dtype),
            jax.ShapeDtypeStruct((n_dp, *down.shape), down.dtype),
        ),
        in_specs=[pl.BlockSpec(memory_space=pl.ANY)] * 4,
        out_specs=[pl.BlockSpec(memory_space=pl.ANY)] * 4,
        scratch_shapes=[pltpu.SemaphoreType.DMA((extent,)) for extent in sems],
        compiler_params=pltpu.CompilerParams(collective_id=0, has_side_effects=True),
        cost_estimate=pl.CostEstimate(flops=0, bytes_accessed=200_000_000, transcendentals=0),
        name="open_gather",
    )(x, dy, up, down)


def total_kernel(n_dp, n_seq, values, out, by_seq, part, by_dp, s_send, s_recv, d_send, d_recv):
    my_dp, my_seq = lax.axis_index("dp"), lax.axis_index("seq")
    seq_peers = [(my_dp, lax.rem(my_seq + step, n_seq)) for step in range(1, n_seq)]
    dp_peers = [(lax.rem(my_dp + step, n_dp), my_seq) for step in range(1, n_dp)]
    greet(seq_peers + dp_peers)
    copies = [
        send(values, by_seq.at[k], s_send.at[k], s_recv.at[k], target)
        for k, target in enumerate(seq_peers)
    ]
    start_all(copies)
    for copy in copies:
        copy.wait()
    part[...] = values[...] + jnp.sum(by_seq[...], axis=0)
    copies = [
        send(part, by_dp.at[k], d_send.at[k], d_recv.at[k], target)
        for k, target in enumerate(dp_peers)
    ]
    start_all(copies)
    for copy in copies:
        copy.wait()
    out[...] = part[...] + jnp.sum(by_dp[...], axis=0)


def total(values, number):
    n_seq, n_dp = lax.axis_size("seq"), lax.axis_size("dp")
    return pl.pallas_call(
        functools.partial(total_kernel, n_dp, n_seq),
        out_shape=jax.ShapeDtypeStruct(values.shape, values.dtype),
        in_specs=[pl.BlockSpec(memory_space=pltpu.VMEM)],
        out_specs=pl.BlockSpec(memory_space=pltpu.VMEM),
        scratch_shapes=[
            pltpu.VMEM((n_seq - 1, *values.shape), values.dtype),
            pltpu.VMEM(values.shape, values.dtype),
            pltpu.VMEM((n_dp - 1, *values.shape), values.dtype),
            pltpu.SemaphoreType.DMA((n_seq - 1,)),
            pltpu.SemaphoreType.DMA((n_seq - 1,)),
            pltpu.SemaphoreType.DMA((n_dp - 1,)),
            pltpu.SemaphoreType.DMA((n_dp - 1,)),
        ],
        compiler_params=pltpu.CompilerParams(collective_id=number, has_side_effects=True),
        cost_estimate=pl.CostEstimate(flops=0, bytes_accessed=40_000_000, transcendentals=0),
        name=f"total_{number}",
    )(values)


def gather_seq(rows, number):
    return exchange(rows, number, True).reshape(-1, rows.shape[-1])


def scatter_seq(rows, number):
    count = lax.axis_size("seq")
    chunks = exchange(rows.reshape(count, -1, rows.shape[-1]), number, False)
    return jnp.sum(chunks.astype(wide), axis=0)


def late_scatter_seq(rows):
    count = lax.axis_size("seq")
    chunks = swap_seq(rows.reshape(count, -1, rows.shape[-1]))
    return jnp.sum(chunks.astype(wide), axis=0)


def swap_seq(chunks):
    return lax.all_to_all(chunks, "seq", split_axis=0, concat_axis=0, tiled=True)


def gather_dp(rows):
    return lax.all_gather(rows, "dp", axis=0, tiled=True)


def scatter_dp(rows):
    return lax.psum_scatter(rows, "dp", scatter_dimension=0, tiled=True)


def attention_forward(q_heads, k_heads, v_heads, slopes, block):
    length = q_heads.shape[1]
    kept, outs = [], []
    for start in range(0, length, block):
        end = start + block
        scores = dot("hqe,hke->hqk", q_heads[:, start:end], k_heads[:, :end]) * HEAD_DIM ** (-0.5)
        q_pos = start + lax.broadcasted_iota(jnp.int32, (block, end), 0)
        k_pos = lax.broadcasted_iota(jnp.int32, (block, end), 1)
        distance = (q_pos - k_pos).astype(wide)
        scores = scores - slopes[:, None, None] * distance[None]
        scores = jnp.where(distance[None] >= 0, scores, negative)
        weights = jnp.exp(scores - jnp.max(scores, axis=-1, keepdims=True))
        total = jnp.sum(weights, axis=-1, keepdims=True)
        probs = (weights * (1.0 / total)).astype(low)
        kept.append(probs)
        outs.append(dot("hqk,hke->hqe", probs, v_heads[:, :end]))
    return jnp.concatenate(outs, axis=1), kept


def attention_backward(q_heads, k_heads, v_heads, g_heads, delta, kept, block):
    length = q_heads.shape[1]
    grad_q = []
    grad_k = jnp.zeros(k_heads.shape, wide)
    grad_v = jnp.zeros(v_heads.shape, wide)
    for index, start in enumerate(range(0, length, block)):
        end = start + block
        probs = kept[index]
        g_blk = g_heads[:, start:end]
        q_blk = q_heads[:, start:end]
        grad_probs = dot("hqe,hke->hqk", g_blk, v_heads[:, :end])
        grad_scores = (
            probs.astype(wide) * (grad_probs - delta[:, start:end, None]) * HEAD_DIM ** (-0.5)
        ).astype(low)
        grad_q.append(dot("hqk,hke->hqe", grad_scores, k_heads[:, :end]))
        grad_k = grad_k.at[:, :end].add(dot("hqk,hqe->hke", grad_scores, q_blk))
        grad_v = grad_v.at[:, :end].add(dot("hqk,hqe->hke", probs, g_blk))
    return jnp.concatenate(grad_q, axis=1), grad_k, grad_v


def body(
    tokens,
    out_grad,
    alibi_slopes,
    qkv_weight,
    dense_weight,
    fc1_weight,
    fc2_weight,
    norm_gains,
    biases,
    fc1_bias,
):
    n_dp, n_seq = lax.axis_size("dp"), lax.axis_size("seq")
    parts = n_dp * n_seq
    my_dp, my_seq = lax.axis_index("dp"), lax.axis_index("seq")
    me = my_dp * n_seq + my_seq
    width = HEADS * HEAD_DIM
    rows, length = tokens.shape[1], tokens.shape[1] * n_seq
    local_heads = HEADS // n_seq
    cols = width // n_seq
    w_rows = qkv_weight.shape[0]
    ff_rows = fc2_weight.shape[0]
    units = ff_rows * n_dp
    block = min(256, length)
    back = [((b % n_dp) * n_seq + b // n_dp, b) for b in range(parts)]

    part_qkv = qkv_weight.reshape(w_rows, 3, n_seq, cols).transpose(2, 0, 1, 3)
    part_fc1 = fc1_weight.reshape(w_rows, n_dp, n_seq, ff_rows).transpose(2, 0, 1, 3)
    small = jnp.concatenate([norm_gains.reshape(-1), biases.reshape(-1), fc1_bias])
    used = 8 * w_rows + ff_rows
    small = jnp.pad(small, (0, w_rows * 128 - used)).reshape(w_rows, 128)
    shared = jnp.concatenate([dense_weight, small], axis=1)
    up = jnp.concatenate(
        [
            part_qkv.reshape(n_seq, w_rows, 3 * cols),
            part_fc1.reshape(n_seq, w_rows, units),
            jnp.broadcast_to(shared[None], (n_seq, *shared.shape)),
        ],
        axis=2,
    )
    dy = out_grad[0]
    x_all, dy_all, up_all, w_fc2 = open_gather(tokens[0], dy, up, fc2_weight)
    up_all = up_all.reshape(width, up.shape[-1])
    marks = (3 * cols, 3 * cols + units, 3 * cols + units + width)
    w_qkv, w_fc1 = up_all[:, : marks[0]], up_all[:, marks[0] : marks[1]]
    w_dense_all = up_all[:, marks[1] : marks[2]]
    w_dense = lax.dynamic_slice_in_dim(w_dense_all, my_seq * cols, cols, 0)
    w_fc2 = w_fc2.reshape(units, width)
    dy_all = dy_all.reshape(length, width)
    small = up_all[:, marks[2] :].reshape(parts, w_rows * 128)[:, :used]
    vec = small[:, : 8 * w_rows].reshape(parts, 8, w_rows).transpose(1, 0, 2).reshape(8, width)
    vec = vec.astype(wide)
    gains, shifts = vec[:2], vec[2:]
    ff_bias = small[:, 8 * w_rows :].reshape(n_dp, n_seq, ff_rows)
    ff_bias = lax.dynamic_index_in_dim(ff_bias, my_seq, 1, keepdims=False).reshape(units)
    ff_bias = ff_bias.astype(wide)

    inputs = tokens[0].astype(wide)
    _, norm_pull_one = jax.vjp(layer_norm, inputs, gains[0], shifts[0])
    x_all = x_all.reshape(length, width).astype(wide)
    h_one = layer_norm(x_all, gains[0], shifts[0]).astype(low)

    def my_cols(row):
        return lax.dynamic_slice_in_dim(row, my_seq * cols, cols, 0)

    proj_bias = jnp.concatenate([my_cols(shifts[1]), jnp.zeros((cols,), wide), my_cols(shifts[2])])
    projected = (dot("td,dc->tc", h_one, w_qkv) + proj_bias).astype(low)
    heads_first = projected.reshape(length, 3, local_heads, HEAD_DIM).transpose(1, 2, 0, 3)
    q_heads, k_heads, v_heads = heads_first[0], heads_first[1], heads_first[2]
    slopes = lax.dynamic_slice_in_dim(alibi_slopes, my_seq * local_heads, local_heads, 0)
    attended, kept = attention_forward(q_heads, k_heads, v_heads, slopes, block)
    attended_low = attended.astype(low).transpose(1, 0, 2).reshape(length, cols)
    o_all = exchange(attended_low, 1, True)
    branch = dot("gtc,gcd->td", o_all, w_dense_all.reshape(n_seq, cols, width))
    residual_all = x_all + branch + shifts[3]
    h_two = layer_norm(residual_all, gains[1], shifts[4]).astype(low)
    residual = lax.dynamic_slice_in_dim(residual_all, my_seq * rows, rows, 0)
    _, norm_pull_two = jax.vjp(layer_norm, residual, gains[1], shifts[4])
    upper = dot("td,df->tf", h_two, w_fc1) + ff_bias
    activated, gelu_pull = jax.vjp(gelu_tanh, upper)
    act_low = activated.astype(low)
    grad_act = dot("td,fd->tf", dy_all, w_fc2)
    grad_upper = gelu_pull(grad_act)[0].astype(low)
    part_h_two = dot("tf,df->td", grad_upper, w_fc1).astype(low)
    part_fc2 = dot("tf,td->fd", act_low, dy_all).astype(low)
    part_fc1 = dot("td,tf->df", h_two, grad_upper).astype(low)
    part_h_two, part_fc2, part_fc1 = lax.optimization_barrier((part_h_two, part_fc2, part_fc1))
    grad_fc2 = scatter_dp(part_fc2)
    grad_fc1 = scatter_dp(part_fc1)
    grad_h_two = scatter_seq(part_h_two, 3)
    part_out = dot("tf,fd->td", act_low, w_fc2).astype(low)
    grad_fc1_bias = jnp.sum(grad_upper, axis=0, dtype=wide)

    grad_res_norm, grad_gain_two, grad_shift_two = norm_pull_two(grad_h_two)
    grad_resid = dy.astype(wide) + grad_res_norm
    grad_branch = grad_resid.astype(low)
    branch_all = gather_seq(grad_branch, 4)
    branch_all, part_out = lax.optimization_barrier((branch_all, part_out))
    layer_out = (residual + late_scatter_seq(part_out) + shifts[5]).astype(low)
    grad_dense = scatter_dp(dot("tc,td->cd", attended_low, branch_all).astype(low))
    grad_attended = dot("td,cd->tc", branch_all, w_dense).astype(low)
    g_heads = grad_attended.reshape(length, local_heads, HEAD_DIM).transpose(1, 0, 2)
    delta = jnp.sum(g_heads.astype(wide) * attended, axis=-1)
    grad_q, grad_k, grad_v = attention_backward(
        q_heads, k_heads, v_heads, g_heads, delta, kept, block
    )
    grad_proj = jnp.stack([grad_q, grad_k, grad_v]).astype(low)
    grad_proj = grad_proj.transpose(2, 0, 1, 3).reshape(length, 3 * cols)
    part_h_one = dot("tc,dc->td", grad_proj, w_qkv).astype(low)
    part_qkv = dot("td,tc->dc", h_one, grad_proj).astype(low)
    part_h_one, part_qkv, grad_fc2, grad_fc1 = lax.optimization_barrier(
        (part_h_one, part_qkv, grad_fc2, grad_fc1)
    )
    grad_qkv = scatter_dp(part_qkv)
    grad_h_one = scatter_seq(part_h_one, 5)
    proj_sums = jnp.sum(grad_proj, axis=0, dtype=wide)

    def place(values):
        return lax.dynamic_update_slice_in_dim(jnp.zeros((width,), wide), values, my_seq * cols, 0)

    grad_in_norm, grad_gain_one, grad_shift_one = norm_pull_one(grad_h_one)
    tokens_grad = (grad_resid + grad_in_norm).astype(low)[None]
    ff_placed = lax.dynamic_update_slice_in_dim(
        jnp.zeros((n_dp, n_seq, ff_rows), wide),
        grad_fc1_bias.reshape(n_dp, 1, ff_rows),
        my_seq,
        1,
    )
    vec_sums = jnp.stack(
        [
            grad_gain_one,
            grad_gain_two,
            grad_shift_one,
            place(proj_sums[:cols]),
            place(proj_sums[2 * cols :]),
            jnp.sum(grad_branch, axis=0, dtype=wide),
            grad_shift_two,
            jnp.sum(dy, axis=0, dtype=wide),
        ]
    )
    sums = jnp.concatenate([vec_sums.reshape(-1, 128), ff_placed.reshape(-1, 128)])
    sums, grad_dense = lax.optimization_barrier((sums, grad_dense))
    sums = total(sums, 6).reshape(-1)
    vec_sums = lax.dynamic_slice_in_dim(sums[: 8 * width].reshape(8, width), me * w_rows, w_rows, 1)
    fc1_bias_grad = lax.dynamic_slice_in_dim(sums, 8 * width + me * ff_rows, ff_rows, 0)

    out_fc1 = swap_seq(grad_fc1.reshape(n_seq, w_rows, units))
    out_fc1 = out_fc1.reshape(n_seq, w_rows, n_dp, ff_rows).transpose(1, 2, 0, 3)
    out_qkv = swap_seq(grad_qkv.reshape(n_seq, w_rows, 3 * cols))
    out_qkv = out_qkv.reshape(n_seq, w_rows, 3, cols).transpose(1, 2, 0, 3)
    out_dense = lax.ppermute(grad_dense, ("dp", "seq"), back)
    return (
        layer_out[None],
        tokens_grad,
        out_qkv.reshape(w_rows, 3 * width).astype(wide),
        out_dense.astype(wide),
        out_fc1.reshape(w_rows, units * n_seq).astype(wide),
        grad_fc2.astype(wide),
        vec_sums[:2],
        vec_sums[2:],
        fc1_bias_grad,
    )


def solution(mesh):
    return jax.shard_map(
        body,
        mesh=mesh,
        in_specs=(
            P("dp", "seq", None),
            P("dp", "seq", None),
            P(),
            P(("dp", "seq"), None),
            P(("dp", "seq"), None),
            P(("dp", "seq"), None),
            P(("dp", "seq"), None),
            P(None, ("dp", "seq")),
            P(None, ("dp", "seq")),
            P(("dp", "seq")),
        ),
        out_specs=(
            P("dp", "seq", None),
            P("dp", "seq", None),
            P(("dp", "seq"), None),
            P(("dp", "seq"), None),
            P(("dp", "seq"), None),
            P(("dp", "seq"), None),
            P(None, ("dp", "seq")),
            P(None, ("dp", "seq")),
            P(("dp", "seq")),
        ),
        check_vma=False,
    )
```

```python
import functools
import jax
import jax.numpy as jnp
from jax import lax
from jax.experimental import pallas as pl
from jax.experimental.pallas import tpu as pltpu
from jax.sharding import PartitionSpec as P

HEADS = 16
HEAD_DIM = 64


epsilon = 1e-05
negative = -1e30
low = jnp.bfloat16
wide = jnp.float32


def layer_norm(values, gain_vec, shift_vec):
    row_mean = jnp.mean(values, axis=-1, keepdims=True)
    centred = values - row_mean
    spread = jnp.mean(centred * centred, axis=-1, keepdims=True)
    return centred * lax.rsqrt(spread + epsilon) * gain_vec + shift_vec


def gelu_tanh(values):
    return jax.nn.gelu(values, approximate=True)


def dot(spec, left, right):
    return jnp.einsum(spec, left, right, preferred_element_type=wide)


def start_all(copies):
    for copy in copies:
        copy.start()


def greet(targets):
    barrier = pltpu.get_barrier_semaphore()
    for target in targets:
        pl.semaphore_signal(barrier, inc=1, device_id=target, device_id_type=pl.DeviceIdType.MESH)
    pl.semaphore_wait(barrier, len(targets))


def send(src, dst, send_sem, recv_sem, target):
    return pltpu.make_async_remote_copy(
        src_ref=src,
        dst_ref=dst,
        send_sem=send_sem,
        recv_sem=recv_sem,
        device_id=target,
        device_id_type=pl.DeviceIdType.MESH,
    )


def exchange_kernel(count, is_gather, src, out, send_sem, recv_sem, local_sem):
    mine, my_dp = lax.axis_index("seq"), lax.axis_index("dp")
    peers = [lax.rem(mine + step, count) for step in range(1, count)]
    greet([(my_dp, peer) for peer in peers])
    copies = [
        send(
            src if is_gather else src.at[peer],
            out.at[mine],
            send_sem.at[step],
            recv_sem.at[step],
            (my_dp, peer),
        )
        for step, peer in enumerate(peers)
    ]
    start_all(copies)
    local = pltpu.make_async_copy(src if is_gather else src.at[mine], out.at[mine], local_sem)
    local.start()
    local.wait()
    for copy in copies:
        copy.wait()


def exchange(values, number, is_gather):
    count = lax.axis_size("seq")
    shape = (count, *values.shape) if is_gather else values.shape
    return pl.pallas_call(
        functools.partial(exchange_kernel, count, is_gather),
        out_shape=jax.ShapeDtypeStruct(shape, values.dtype),
        in_specs=[pl.BlockSpec(memory_space=pl.ANY)],
        out_specs=pl.BlockSpec(memory_space=pl.ANY),
        scratch_shapes=[
            pltpu.SemaphoreType.DMA((count - 1,)),
            pltpu.SemaphoreType.DMA((count - 1,)),
            pltpu.SemaphoreType.DMA,
        ],
        compiler_params=pltpu.CompilerParams(collective_id=number, has_side_effects=True),
        cost_estimate=pl.CostEstimate(flops=0, bytes_accessed=60_000_000, transcendentals=0),
        name=f"exchange_{number}",
    )(values)


def open_kernel(
    n_z, n_seq, x, dy, up, down, x_all, dy_all, up_all, down_all,
    swap_s, swap_r, x_s, x_r, dy_s, dy_r, up_s, up_r, down_s, down_r, up_ts, up_tr, down_ts, down_tr,
    local_sem,
):
    my_dp, my_seq = lax.axis_index("dp"), lax.axis_index("seq")
    my_z, core = my_dp // 2, lax.rem(my_dp, 2)
    seq_peers = [lax.rem(my_seq + step, n_seq) for step in range(1, n_seq)]
    z_peers = [(lax.rem(my_z + step, n_z) * 2 + core, my_seq) for step in range(1, n_z)]
    twin = (my_z * 2 + 1 - core, my_seq)
    greet([(my_dp, peer) for peer in seq_peers] + z_peers + [twin])
    swaps = [
        send(up.at[p], up_all.at[my_dp, my_seq], swap_s.at[k], swap_r.at[k], (my_dp, p))
        for k, p in enumerate(seq_peers)
    ]
    start_all(swaps)
    downs = [
        send(down, down_all.at[my_dp], down_s.at[k], down_r.at[k], target)
        for k, target in enumerate(z_peers)
    ]
    start_all(downs)
    down_twins = [send(down, down_all.at[my_dp], down_ts.at[0], down_tr.at[0], twin)]
    start_all(down_twins)
    rows = []
    for k, p in enumerate(seq_peers):
        rows.append(send(x, x_all.at[my_seq], x_s.at[k], x_r.at[k], (my_dp, p)))
        rows.append(send(dy, dy_all.at[my_seq], dy_s.at[k], dy_r.at[k], (my_dp, p)))
    start_all(rows)
    own = [
        pltpu.make_async_copy(up.at[my_seq], up_all.at[my_dp, my_seq], local_sem.at[0]),
        pltpu.make_async_copy(down, down_all.at[my_dp], local_sem.at[1]),
        pltpu.make_async_copy(x, x_all.at[my_seq], local_sem.at[2]),
        pltpu.make_async_copy(dy, dy_all.at[my_seq], local_sem.at[3]),
    ]
    start_all(own)
    for copy in own:
        copy.wait()
    for copy in swaps:
        copy.wait()
    ups = [
        send(up_all.at[my_dp], up_all.at[my_dp], up_s.at[k], up_r.at[k], target)
        for k, target in enumerate(z_peers)
    ]
    start_all(ups)
    up_twins = [send(up_all.at[my_dp], up_all.at[my_dp], up_ts.at[0], up_tr.at[0], twin)]
    start_all(up_twins)
    for copies, onward, whole, send_sem, recv_sem in (
        (downs, down_twins, down_all, down_ts, down_tr),
        (ups, up_twins, up_all, up_ts, up_tr),
    ):
        for k in range(1, n_z):
            copies[k - 1].wait_recv()
            slot = lax.rem(my_z + n_z - k, n_z) * 2 + core
            onward.append(send(whole.at[slot], whole.at[slot], send_sem.at[k], recv_sem.at[k], twin))
            onward[-1].start()
    for copy in downs + ups:
        copy.wait_send()
    for copy in down_twins + up_twins + rows:
        copy.wait()


def open_gather(x, dy, up, down):
    n_seq, n_dp = lax.axis_size("seq"), lax.axis_size("dp")
    n_z = n_dp // 2
    sems = [n_seq - 1] * 6 + [n_z - 1] * 4 + [n_z] * 4 + [4]
    return pl.pallas_call(
        functools.partial(open_kernel, n_z, n_seq),
        out_shape=(
            jax.ShapeDtypeStruct((n_seq, *x.shape), x.dtype),
            jax.ShapeDtypeStruct((n_seq, *dy.shape), dy.dtype),
            jax.ShapeDtypeStruct((n_dp, *up.shape), up.dtype),
            jax.ShapeDtypeStruct((n_dp, *down.shape), down.dtype),
        ),
        in_specs=[pl.BlockSpec(memory_space=pl.ANY)] * 4,
        out_specs=[pl.BlockSpec(memory_space=pl.ANY)] * 4,
        scratch_shapes=[pltpu.SemaphoreType.DMA((extent,)) for extent in sems],
        compiler_params=pltpu.CompilerParams(collective_id=0, has_side_effects=True),
        cost_estimate=pl.CostEstimate(flops=0, bytes_accessed=200_000_000, transcendentals=0),
        name="open_gather",
    )(x, dy, up, down)


def total_kernel(n_dp, n_seq, values, out, by_seq, part, by_dp, s_send, s_recv, d_send, d_recv):
    my_dp, my_seq = lax.axis_index("dp"), lax.axis_index("seq")
    seq_peers = [(my_dp, lax.rem(my_seq + step, n_seq)) for step in range(1, n_seq)]
    dp_peers = [(lax.rem(my_dp + step, n_dp), my_seq) for step in range(1, n_dp)]
    greet(seq_peers + dp_peers)
    copies = [
        send(values, by_seq.at[k], s_send.at[k], s_recv.at[k], target)
        for k, target in enumerate(seq_peers)
    ]
    start_all(copies)
    for copy in copies:
        copy.wait()
    part[...] = values[...] + jnp.sum(by_seq[...], axis=0)
    copies = [
        send(part, by_dp.at[k], d_send.at[k], d_recv.at[k], target)
        for k, target in enumerate(dp_peers)
    ]
    start_all(copies)
    for copy in copies:
        copy.wait()
    out[...] = part[...] + jnp.sum(by_dp[...], axis=0)


def total(values, number):
    n_seq, n_dp = lax.axis_size("seq"), lax.axis_size("dp")
    return pl.pallas_call(
        functools.partial(total_kernel, n_dp, n_seq),
        out_shape=jax.ShapeDtypeStruct(values.shape, values.dtype),
        in_specs=[pl.BlockSpec(memory_space=pltpu.VMEM)],
        out_specs=pl.BlockSpec(memory_space=pltpu.VMEM),
        scratch_shapes=[
            pltpu.VMEM((n_seq - 1, *values.shape), values.dtype),
            pltpu.VMEM(values.shape, values.dtype),
            pltpu.VMEM((n_dp - 1, *values.shape), values.dtype),
            pltpu.SemaphoreType.DMA((n_seq - 1,)),
            pltpu.SemaphoreType.DMA((n_seq - 1,)),
            pltpu.SemaphoreType.DMA((n_dp - 1,)),
            pltpu.SemaphoreType.DMA((n_dp - 1,)),
        ],
        compiler_params=pltpu.CompilerParams(collective_id=number, has_side_effects=True),
        cost_estimate=pl.CostEstimate(flops=0, bytes_accessed=40_000_000, transcendentals=0),
        name=f"total_{number}",
    )(values)


def gather_seq(rows, number):
    return exchange(rows, number, True).reshape(-1, rows.shape[-1])


def scatter_seq(rows, number):
    count = lax.axis_size("seq")
    chunks = exchange(rows.reshape(count, -1, rows.shape[-1]), number, False)
    return jnp.sum(chunks.astype(wide), axis=0)


def late_scatter_seq(rows):
    return lax.psum_scatter(rows, "seq", scatter_dimension=0, tiled=True)


def swap_seq(chunks):
    return lax.all_to_all(chunks, "seq", split_axis=0, concat_axis=0, tiled=True)


def gather_dp(rows):
    return lax.all_gather(rows, "dp", axis=0, tiled=True)


def scatter_dp(rows):
    return lax.psum_scatter(rows, "dp", scatter_dimension=0, tiled=True)


def attention_forward(q_heads, k_heads, v_heads, slopes, block):
    length = q_heads.shape[1]
    kept, outs = [], []
    for start in range(0, length, block):
        end = start + block
        scores = dot("hqe,hke->hqk", q_heads[:, start:end], k_heads[:, :end]) * HEAD_DIM ** (-0.5)
        q_pos = start + lax.broadcasted_iota(jnp.int32, (block, end), 0)
        k_pos = lax.broadcasted_iota(jnp.int32, (block, end), 1)
        distance = (q_pos - k_pos).astype(wide)
        scores = scores - slopes[:, None, None] * distance[None]
        scores = jnp.where(distance[None] >= 0, scores, negative)
        weights = jnp.exp(scores - jnp.max(scores, axis=-1, keepdims=True))
        total = jnp.sum(weights, axis=-1, keepdims=True)
        probs = (weights * (1.0 / total)).astype(low)
        kept.append(probs)
        outs.append(dot("hqk,hke->hqe", probs, v_heads[:, :end]))
    return jnp.concatenate(outs, axis=1), kept


def attention_backward(q_heads, k_heads, v_heads, g_heads, delta, kept, block):
    length = q_heads.shape[1]
    grad_q = []
    grad_k = jnp.zeros(k_heads.shape, wide)
    grad_v = jnp.zeros(v_heads.shape, wide)
    for index, start in enumerate(range(0, length, block)):
        end = start + block
        probs = kept[index]
        g_blk = g_heads[:, start:end]
        q_blk = q_heads[:, start:end]
        grad_probs = dot("hqe,hke->hqk", g_blk, v_heads[:, :end])
        grad_scores = (
            probs.astype(wide) * (grad_probs - delta[:, start:end, None]) * HEAD_DIM ** (-0.5)
        ).astype(low)
        grad_q.append(dot("hqk,hke->hqe", grad_scores, k_heads[:, :end]))
        grad_k = grad_k.at[:, :end].add(dot("hqk,hqe->hke", grad_scores, q_blk))
        grad_v = grad_v.at[:, :end].add(dot("hqk,hqe->hke", probs, g_blk))
    return jnp.concatenate(grad_q, axis=1), grad_k, grad_v


def body(
    tokens,
    out_grad,
    alibi_slopes,
    qkv_weight,
    dense_weight,
    fc1_weight,
    fc2_weight,
    norm_gains,
    biases,
    fc1_bias,
):
    n_dp, n_seq = lax.axis_size("dp"), lax.axis_size("seq")
    parts = n_dp * n_seq
    my_dp, my_seq = lax.axis_index("dp"), lax.axis_index("seq")
    me = my_dp * n_seq + my_seq
    width = HEADS * HEAD_DIM
    rows, length = tokens.shape[1], tokens.shape[1] * n_seq
    local_heads = HEADS // n_seq
    cols = width // n_seq
    w_rows = qkv_weight.shape[0]
    ff_rows = fc2_weight.shape[0]
    units = ff_rows * n_dp
    block = min(256, length)
    back = [((b % n_dp) * n_seq + b // n_dp, b) for b in range(parts)]

    part_qkv = qkv_weight.reshape(w_rows, 3, n_seq, cols).transpose(2, 0, 1, 3)
    part_fc1 = fc1_weight.reshape(w_rows, n_dp, n_seq, ff_rows).transpose(2, 0, 1, 3)
    small = jnp.concatenate([norm_gains.reshape(-1), biases.reshape(-1), fc1_bias])
    used = 8 * w_rows + ff_rows
    small = jnp.pad(small, (0, w_rows * 128 - used)).reshape(w_rows, 128)
    shared = jnp.concatenate([dense_weight, small], axis=1)
    up = jnp.concatenate(
        [
            part_qkv.reshape(n_seq, w_rows, 3 * cols),
            part_fc1.reshape(n_seq, w_rows, units),
            jnp.broadcast_to(shared[None], (n_seq, *shared.shape)),
        ],
        axis=2,
    )
    dy = out_grad[0]
    x_all, dy_all, up_all, w_fc2 = open_gather(tokens[0], dy, up, fc2_weight)
    up_all = up_all.reshape(width, up.shape[-1])
    marks = (3 * cols, 3 * cols + units, 3 * cols + units + width)
    w_qkv, w_fc1 = up_all[:, : marks[0]], up_all[:, marks[0] : marks[1]]
    w_dense_all = up_all[:, marks[1] : marks[2]]
    w_dense = lax.dynamic_slice_in_dim(w_dense_all, my_seq * cols, cols, 0)
    w_fc2 = w_fc2.reshape(units, width)
    dy_all = dy_all.reshape(length, width)
    small = up_all[:, marks[2] :].reshape(parts, w_rows * 128)[:, :used]
    vec = small[:, : 8 * w_rows].reshape(parts, 8, w_rows).transpose(1, 0, 2).reshape(8, width)
    vec = vec.astype(wide)
    gains, shifts = vec[:2], vec[2:]
    ff_bias = small[:, 8 * w_rows :].reshape(n_dp, n_seq, ff_rows)
    ff_bias = lax.dynamic_index_in_dim(ff_bias, my_seq, 1, keepdims=False).reshape(units)
    ff_bias = ff_bias.astype(wide)

    inputs = tokens[0].astype(wide)
    _, norm_pull_one = jax.vjp(layer_norm, inputs, gains[0], shifts[0])
    x_all = x_all.reshape(length, width).astype(wide)
    h_one = layer_norm(x_all, gains[0], shifts[0]).astype(low)

    def my_cols(row):
        return lax.dynamic_slice_in_dim(row, my_seq * cols, cols, 0)

    proj_bias = jnp.concatenate([my_cols(shifts[1]), jnp.zeros((cols,), wide), my_cols(shifts[2])])
    projected = (dot("td,dc->tc", h_one, w_qkv) + proj_bias).astype(low)
    heads_first = projected.reshape(length, 3, local_heads, HEAD_DIM).transpose(1, 2, 0, 3)
    q_heads, k_heads, v_heads = heads_first[0], heads_first[1], heads_first[2]
    slopes = lax.dynamic_slice_in_dim(alibi_slopes, my_seq * local_heads, local_heads, 0)
    attended, kept = attention_forward(q_heads, k_heads, v_heads, slopes, block)
    attended_low = attended.astype(low).transpose(1, 0, 2).reshape(length, cols)
    o_all = exchange(attended_low, 1, True)
    branch = dot("gtc,gcd->td", o_all, w_dense_all.reshape(n_seq, cols, width))
    residual_all = x_all + branch + shifts[3]
    h_two = layer_norm(residual_all, gains[1], shifts[4]).astype(low)
    residual = lax.dynamic_slice_in_dim(residual_all, my_seq * rows, rows, 0)
    _, norm_pull_two = jax.vjp(layer_norm, residual, gains[1], shifts[4])
    upper = dot("td,df->tf", h_two, w_fc1) + ff_bias
    activated, gelu_pull = jax.vjp(gelu_tanh, upper)
    act_low = activated.astype(low)
    part_out = dot("tf,fd->td", act_low, w_fc2).astype(low)
    part_out, dy_all = lax.optimization_barrier((part_out, dy_all))
    out_sum = late_scatter_seq(part_out)
    grad_act = dot("td,fd->tf", dy_all, w_fc2)
    grad_upper = gelu_pull(grad_act)[0].astype(low)
    part_h_two = dot("tf,df->td", grad_upper, w_fc1).astype(low)
    part_fc2 = dot("tf,td->fd", act_low, dy_all).astype(low)
    part_fc1 = dot("td,tf->df", h_two, grad_upper).astype(low)
    part_h_two, part_fc2, part_fc1, out_sum = lax.optimization_barrier(
        (part_h_two, part_fc2, part_fc1, out_sum)
    )
    layer_out = (residual + out_sum.astype(wide) + shifts[5]).astype(low)
    grad_fc2 = scatter_dp(part_fc2)
    grad_fc1 = scatter_dp(part_fc1)
    grad_h_two = scatter_seq(part_h_two, 3)
    grad_fc1_bias = jnp.sum(grad_upper, axis=0, dtype=wide)

    grad_res_norm, grad_gain_two, grad_shift_two = norm_pull_two(grad_h_two)
    grad_resid = dy.astype(wide) + grad_res_norm
    grad_branch = grad_resid.astype(low)
    branch_all = gather_seq(grad_branch, 4)
    grad_dense = scatter_dp(dot("tc,td->cd", attended_low, branch_all).astype(low))
    grad_attended = dot("td,cd->tc", branch_all, w_dense).astype(low)
    g_heads = grad_attended.reshape(length, local_heads, HEAD_DIM).transpose(1, 0, 2)
    delta = jnp.sum(g_heads.astype(wide) * attended, axis=-1)
    grad_q, grad_k, grad_v = attention_backward(
        q_heads, k_heads, v_heads, g_heads, delta, kept, block
    )
    grad_proj = jnp.stack([grad_q, grad_k, grad_v]).astype(low)
    grad_proj = grad_proj.transpose(2, 0, 1, 3).reshape(length, 3 * cols)
    part_h_one = dot("tc,dc->td", grad_proj, w_qkv).astype(low)
    part_qkv = dot("td,tc->dc", h_one, grad_proj).astype(low)
    part_h_one, part_qkv, grad_fc2, grad_fc1 = lax.optimization_barrier(
        (part_h_one, part_qkv, grad_fc2, grad_fc1)
    )
    grad_qkv = scatter_dp(part_qkv)
    grad_h_one = scatter_seq(part_h_one, 5)
    proj_sums = jnp.sum(grad_proj, axis=0, dtype=wide)

    def place(values):
        return lax.dynamic_update_slice_in_dim(jnp.zeros((width,), wide), values, my_seq * cols, 0)

    grad_in_norm, grad_gain_one, grad_shift_one = norm_pull_one(grad_h_one)
    tokens_grad = (grad_resid + grad_in_norm).astype(low)[None]
    ff_placed = lax.dynamic_update_slice_in_dim(
        jnp.zeros((n_dp, n_seq, ff_rows), wide),
        grad_fc1_bias.reshape(n_dp, 1, ff_rows),
        my_seq,
        1,
    )
    vec_sums = jnp.stack(
        [
            grad_gain_one,
            grad_gain_two,
            grad_shift_one,
            place(proj_sums[:cols]),
            place(proj_sums[2 * cols :]),
            jnp.sum(grad_branch, axis=0, dtype=wide),
            grad_shift_two,
            jnp.sum(dy, axis=0, dtype=wide),
        ]
    )
    sums = jnp.concatenate([vec_sums.reshape(-1, 128), ff_placed.reshape(-1, 128)])
    sums, grad_dense = lax.optimization_barrier((sums, grad_dense))
    sums = total(sums, 6).reshape(-1)
    vec_sums = lax.dynamic_slice_in_dim(sums[: 8 * width].reshape(8, width), me * w_rows, w_rows, 1)
    fc1_bias_grad = lax.dynamic_slice_in_dim(sums, 8 * width + me * ff_rows, ff_rows, 0)

    out_fc1 = swap_seq(grad_fc1.reshape(n_seq, w_rows, units))
    out_fc1 = out_fc1.reshape(n_seq, w_rows, n_dp, ff_rows).transpose(1, 2, 0, 3)
    out_qkv = swap_seq(grad_qkv.reshape(n_seq, w_rows, 3 * cols))
    out_qkv = out_qkv.reshape(n_seq, w_rows, 3, cols).transpose(1, 2, 0, 3)
    out_dense = lax.ppermute(grad_dense, ("dp", "seq"), back)
    return (
        layer_out[None],
        tokens_grad,
        out_qkv.reshape(w_rows, 3 * width).astype(wide),
        out_dense.astype(wide),
        out_fc1.reshape(w_rows, units * n_seq).astype(wide),
        grad_fc2.astype(wide),
        vec_sums[:2],
        vec_sums[2:],
        fc1_bias_grad,
    )


def solution(mesh):
    return jax.shard_map(
        body,
        mesh=mesh,
        in_specs=(
            P("dp", "seq", None),
            P("dp", "seq", None),
            P(),
            P(("dp", "seq"), None),
            P(("dp", "seq"), None),
            P(("dp", "seq"), None),
            P(("dp", "seq"), None),
            P(None, ("dp", "seq")),
            P(None, ("dp", "seq")),
            P(("dp", "seq")),
        ),
        out_specs=(
            P("dp", "seq", None),
            P("dp", "seq", None),
            P(("dp", "seq"), None),
            P(("dp", "seq"), None),
            P(("dp", "seq"), None),
            P(("dp", "seq"), None),
            P(None, ("dp", "seq")),
            P(None, ("dp", "seq")),
            P(("dp", "seq")),
        ),
        check_vma=False,
    )
```
